512 devices in a mesh: dp: 32 (over z_lo, y, core), tensor: 16 (over x, z_hi).
Axes of the slice: x: 4, y: 8, z: 8 (z_hi: 4, z_lo: 2; z = z_hi * 2 + z_lo), core: 2. Of those that a mesh axis runs over, the one named last changes fastest.
Arguments:
- queries: bfloat16 [16384, 8192], P('dp', 'tensor'), may hold values from -5 to 5
- keys: bfloat16 [16384, 1024], P('dp', 'tensor'), may hold values from -5 to 5
- values: bfloat16 [16384, 1024], P('dp', 'tensor'), may hold values from -6 to 6
- grad_out: bfloat16 [16384, 4096], P(('dp', 'tensor')), may hold values from -6 to 6
- out_weight: bfloat16 [4096, 8192], P('dp', 'tensor'), may hold values from -0.375 to 0.375
Outputs:
- grad_queries: bfloat16 [16384, 8192], P('dp', 'tensor')
- grad_keys: bfloat16 [16384, 1024], P('dp', 'tensor')
- grad_values: bfloat16 [16384, 1024], P('dp', 'tensor')
- grad_weight: bfloat16 [4096, 8192], P('dp', 'tensor')
The draws below stay inside these ranges and needn't reach their ends.
All inputs are finite; a program needn't handle non-finite values.
Results may differ from the reference program's by a relative error of at most 0.03.
Values may be sent and summed in bfloat16 or wider, within the bound.
A program may use at most 64 MiB of HBM per device.

```python
import jax
import jax.numpy as jnp
from jax import lax

HEAD_DIM = 128
HEADS_DEV = 4
WIDTH = 4096
SEQ = 512
HEADS = 64
KV_HEADS = 8
TOKENS = 16384
N_DP = 32


def draw_queries(key, part):
    key = jax.random.fold_in(key, 11)
    shape = (TOKENS, HEADS * HEAD_DIM)
    base = jax.random.truncated_normal(key, -4.5, 4.5, shape, jnp.float32)
    return base.astype(jnp.bfloat16)


def draw_keys(key, part):
    key = jax.random.fold_in(key, 23)
    shape = (TOKENS, KV_HEADS * HEAD_DIM)
    base = jax.random.truncated_normal(key, -4.5, 4.5, shape, jnp.float32)
    return base.astype(jnp.bfloat16)


def strengthened(array, own_key, source, target, blocks, factor):
    def block_of(axis_at):
        return (jnp.arange(array.shape[axis_at]) // (array.shape[axis_at] // blocks)).reshape((-1,) + (1,) * (array.ndim - 1 - axis_at))

    first = jax.random.permutation(own_key, blocks)[block_of(target)]
    second = (block_of(target) + blocks // 2) % blocks
    return jnp.where((block_of(source) == first) | (block_of(source) == second), factor * array, array)


def levels(own_key, extent, split, low, top_value):
    def one(axis_at, shards_of):
        heights = jax.random.uniform(jax.random.fold_in(jax.random.fold_in(own_key, 6), axis_at), (shards_of,), jnp.float32, low / len(split), top_value / len(split))
        return jnp.repeat(jnp.exp(heights), extent[axis_at] // shards_of).reshape((-1,) + (1,) * (len(extent) - axis_at - 1))

    factor_of = one(*split[0])
    for cut in split[1:]:
        factor_of = factor_of * one(*cut)
    return factor_of


def noise(key, extent, deviation, bound, split=(), kind=jnp.bfloat16):
    values = deviation * jax.random.normal(key, extent, jnp.float32)
    if split:
        values = values * levels(key, extent, split, -0.22, 0.18)
    return jnp.clip(values, -bound, bound).astype(kind)


def noise_with(own_key, dims, scale, most, split, heavy, kind=jnp.bfloat16):
    array = scale * jax.random.normal(own_key, dims, jnp.float32)
    if split:
        array = array * levels(own_key, dims, split, -0.22, 0.18)
    return jnp.clip(strengthened(array, jax.random.fold_in(own_key, 3), *heavy), -most, most).astype(kind)


def setup_inputs(seed: int = 0) -> dict:
    arg_keys = jax.random.split(jax.random.key(seed), 6)
    return {
        "queries": draw_queries(jax.random.fold_in(arg_keys[5], 71), 0),
        "keys": draw_keys(jax.random.fold_in(arg_keys[5], 71), 0),
        "values": noise(arg_keys[2], (TOKENS, KV_HEADS * HEAD_DIM), 1.0, 6.0, ((0, 32), (1, 16))),
        "grad_out": noise_with(arg_keys[3], (TOKENS, WIDTH), 0.25, 6.0, ((0, 512),), (0, 1, 512, 6.0)),
        "out_weight": noise(arg_keys[4], (WIDTH, HEADS * HEAD_DIM), (WIDTH // 16) ** -0.5, 0.375, ((0, 32), (1, 16))),
    }


def rounded(value):
    return lax.optimization_barrier(value.astype(jnp.bfloat16)).astype(jnp.float32)


def reference(queries, keys, values, grad_out, out_weight):
    scale = HEAD_DIM ** -0.5
    query_seqs = queries.reshape(N_DP, SEQ, HEADS * HEAD_DIM)
    key_seqs = keys.reshape(N_DP, SEQ, KV_HEADS * HEAD_DIM)
    value_seqs = values.reshape(N_DP, SEQ, KV_HEADS * HEAD_DIM)
    grad_seqs = grad_out.reshape(N_DP, SEQ, WIDTH)
    positions = jnp.arange(SEQ, dtype=jnp.int32)
    causal = positions[None, :] <= positions[:, None]

    def sequence_grads(carry, inputs):
        query, key_rows, value_rows, grad_rows = inputs
        query_f = query.astype(jnp.float32).reshape(SEQ, KV_HEADS, 2, HEADS_DEV, HEAD_DIM)
        key_f = key_rows.astype(jnp.float32).reshape(SEQ, KV_HEADS, HEAD_DIM)
        value_f = value_rows.astype(jnp.float32).reshape(SEQ, KV_HEADS, HEAD_DIM)
        scores = jnp.einsum("sgpmd,tgd->gpmst", query_f, key_f) * scale
        scores = jnp.where(causal, scores, -jnp.inf)
        probs = jax.nn.softmax(scores, axis=-1)
        probs_half = probs.astype(jnp.bfloat16).astype(jnp.float32)
        attended = jnp.einsum("gpmst,tgd->sgpmd", probs_half, value_f).astype(jnp.bfloat16)
        attended = attended.reshape(SEQ, HEADS * HEAD_DIM)
        grad_att = jnp.dot(grad_rows, out_weight, preferred_element_type=jnp.float32).astype(jnp.bfloat16)
        grad_att_f = grad_att.astype(jnp.float32).reshape(SEQ, KV_HEADS, 2, HEADS_DEV, HEAD_DIM)
        dprobs = jnp.einsum("sgpmd,tgd->gpmst", grad_att_f, value_f)
        delta = jnp.sum(probs * dprobs, axis=-1, keepdims=True)
        dscores = (probs * (dprobs - delta) * scale).astype(jnp.bfloat16).astype(jnp.float32)
        grad_q = jnp.einsum("gpmst,tgd->sgpmd", dscores, key_f).astype(jnp.bfloat16)
        key_part = rounded(jnp.einsum("gpmst,sgpmd->tgpd", dscores, query_f))
        value_part = rounded(jnp.einsum("gpmst,sgpmd->tgpd", probs_half, grad_att_f))
        grad_k = jnp.sum(key_part, axis=2).astype(jnp.bfloat16).reshape(SEQ, KV_HEADS * HEAD_DIM)
        grad_v = jnp.sum(value_part, axis=2).astype(jnp.bfloat16).reshape(SEQ, KV_HEADS * HEAD_DIM)
        term = lax.dot_general(grad_rows, attended, (((0,), (0,)), ((), ())), preferred_element_type=jnp.float32)
        carry = carry + rounded(term)
        return carry, (grad_q.reshape(SEQ, HEADS * HEAD_DIM), grad_k, grad_v)

    start = jnp.zeros((WIDTH, HEADS * HEAD_DIM), jnp.float32)
    total, (grad_q, grad_k, grad_v) = lax.scan(sequence_grads, start, (query_seqs, key_seqs, value_seqs, grad_seqs))
    grad_queries = grad_q.reshape(TOKENS, HEADS * HEAD_DIM)
    grad_keys = grad_k.reshape(TOKENS, KV_HEADS * HEAD_DIM)
    grad_values = grad_v.reshape(TOKENS, KV_HEADS * HEAD_DIM)
    return grad_queries, grad_keys, grad_values, total.astype(jnp.bfloat16)
```

```python
import jax
import jax.numpy as jnp
from jax import lax
from jax.experimental import pallas as pl
from jax.experimental.pallas import tpu as pltpu
from jax.sharding import PartitionSpec as P

HEAD_DIM = 128
MESH = pl.DeviceIdType.MESH
F32 = jnp.float32
BF16 = jnp.bfloat16

ORDER = (4, 3, -3, 2, -2, 1, -1, 0)
AT = {relative: place for place, relative in enumerate(ORDER)}
AT[-4] = AT[4]
ABOVE = 8

NX, NZ, NY = 4, 4, 8
N_COPIES = 160


def nt(a, b):
    return lax.dot_general(a, b, (((1,), (1,)), ((), ())), preferred_element_type=F32)


def nn(a, b):
    return lax.dot_general(a, b, (((1,), (0,)), ((), ())), preferred_element_type=F32)


def kernel(
    q_ref, k_ref, v_ref, g_ref, w_ref,
    gq_ref, gk_ref, gv_ref, gw_ref,
    gbuf, wbuf, kv_send, kv_recv, k_full, v_full, k_turned, v_turned,
    probs, att, total, grad_att, terms, core_send, core_recv, y_send, y_recv,
    z_send, z_recv, key_acc, value_acc, part_send, part_recv, send_sem, recv_sem,
):
    scale = HEAD_DIM ** (-0.5)
    dp = lax.axis_index("dp")
    tensor = lax.axis_index("tensor")
    core = lax.rem(dp, 2)
    y = lax.rem(dp // 2, NY)
    zl = dp // (2 * NY)
    x = tensor // NZ
    zh = lax.rem(tensor, NZ)
    parity = lax.rem(tensor, 2)

    def device(core=core, y=y, zl=zl, x=x, zh=zh):
        return ((zl * NY + y) * 2 + core, x * NZ + zh)

    x_up, x_down = lax.rem(x + 1, NX), lax.rem(x + NX - 1, NX)
    z_up, z_down = lax.rem(zh + 1, NZ), lax.rem(zh + NZ - 1, NZ)
    to_x_up, to_x_down = device(x=x_up), device(x=x_down)
    to_z_up, to_z_down = device(zh=z_up), device(zh=z_down)
    to_y_up = device(y=lax.rem(y + 1, NY))
    to_y_down = device(y=lax.rem(y + NY - 1, NY))
    to_pair = device(zl=1 - zl)
    to_core = device(core=1 - core)
    to_partner = (dp, tensor + 1 - 2 * parity)

    barrier = pltpu.get_barrier_semaphore()
    for target in (to_x_up, to_x_down, to_z_up, to_z_down, to_y_up, to_y_down, to_pair, to_core):
        pl.semaphore_signal(barrier, inc=1, device_id=target, device_id_type=MESH)

    copies, started = {}, []

    def send(name, source, target, to):
        index = len(started)
        started.append(name)
        copy = pltpu.make_async_remote_copy(
            src_ref=source, dst_ref=target, send_sem=send_sem.at[index], recv_sem=recv_sem.at[index],
            device_id=to, device_id_type=MESH,
        )
        copy.start()
        copies[name] = copy

    def arrived(name):
        copies[name].wait_recv()

    kv_send[...] = jnp.concatenate([k_ref[...], v_ref[...]], 1)
    wbuf[AT[0], 2 + zl] = w_ref[...]
    own_rows = pl.ds(pl.multiple_of(zh * 32, 32), 32)
    for place, relative in enumerate(ORDER):
        column = lax.rem(y + relative + NY, NY)
        for slot in range(4):
            of_core = core if slot >= 2 else 1 - core
            block = ((slot % 2) * NY + column) * 2 + of_core
            gbuf[place, x, own_rows, slot * 128 : (slot + 1) * 128] = g_ref[
                :, pl.ds(pl.multiple_of(block * 128, 128), 128)
            ]
    pl.semaphore_wait(barrier, 8)

    def z_rows(at, first, count):
        return pl.ds(pl.multiple_of(at * 32 + first, 16), count)

    def g_z1(place):
        block = gbuf.at[place, x, z_rows(zh, 0, 32)]
        send(("z1u", place), block, block, to_z_up)
        send(("z1d", place), block, block, to_z_down)

    def g_z2(place):
        arrived(("z1u", place))
        block = gbuf.at[place, x, z_rows(z_down, 0, 16)]
        send(("z2u", place), block, block, to_z_up)
        arrived(("z1d", place))
        block = gbuf.at[place, x, z_rows(z_up, 16, 16)]
        send(("z2d", place), block, block, to_z_down)

    def g_x1(place):
        arrived(("z2u", place))
        arrived(("z2d", place))
        block = gbuf.at[place, x]
        send(("x1u", place), block, block, to_x_up)
        send(("x1d", place), block, block, to_x_down)

    def g_x2(place):
        arrived(("x1u", place))
        block = gbuf.at[place, x_down, 0:64]
        send(("x2u", place), block, block, to_x_up)
        arrived(("x1d", place))
        block = gbuf.at[place, x_up, 64:128]
        send(("x2d", place), block, block, to_x_down)

    def g_done(place):
        arrived(("x2u", place))
        arrived(("x2d", place))

    row = {"a": 2 + zl, "b": 3 - zl}

    def w_hop(block, step, up):
        relative = (1 - step) if up else (step - 1)
        source = wbuf.at[AT[relative], row[block]]
        target = wbuf.at[AT[relative - 1 if up else relative + 1], row[block]]
        send(("w", block, step, up), source, target, to_y_up if up else to_y_down)

    def w_start():
        w_hop("a", 1, True)
        w_hop("a", 1, False)
        own = wbuf.at[AT[0], row["a"]]
        send("wz", own, own, to_pair)

    def w_core(relative):
        send(
            ("wc", AT[relative]), wbuf.at[AT[relative], 2:4], wbuf.at[AT[relative], 0:2], to_core
        )

    def w_pair():
        arrived("wz")
        w_hop("b", 1, True)
        w_hop("b", 1, False)
        w_core(0)

    def w_next(block, step):
        for up in (True, False):
            arrived(("w", block, step, up))
            if step < 3 or (block == "a") == up:
                w_hop(block, step + 1, up)
        if block == "b":
            w_core(step)
            w_core(-step)

    def w_last():
        arrived(("w", "a", 4, True))
        arrived(("w", "b", 4, False))
        w_core(4)

    def spans():
        for part in range(2):
            yield slice(part * 256, part * 256 + 256), (part + 1) * 256

    def kv_ready():
        arrived("kv")
        first = jnp.where(parity == 0, kv_send[...], kv_recv[...])
        second = jnp.where(parity == 0, kv_recv[...], kv_send[...])
        key = jnp.concatenate([first[:, 0:64], second[:, 0:64]], 1)
        value = jnp.concatenate([first[:, 64:128], second[:, 64:128]], 1)
        k_full[...] = key
        v_full[...] = value
        k_turned[...] = key.astype(F32).T.astype(BF16)
        v_turned[...] = value.astype(F32).T.astype(BF16)

    def forward(head):
        columns = slice(head * 128, head * 128 + 128)
        for span, length in spans():
            scores = nt(k_full[0:length], q_ref[span, columns]) * scale
            key_at = lax.broadcasted_iota(jnp.int32, (length, 256), 0)
            query_at = lax.broadcasted_iota(jnp.int32, (length, 256), 1) + (length - 256)
            scores = jnp.where(key_at <= query_at, scores, -jnp.inf)
            powers = jnp.exp(scores - jnp.max(scores, axis=0, keepdims=True))
            part = powers * (1.0 / jnp.sum(powers, axis=0, keepdims=True))
            probs[head, 0:length, span] = part
            att[columns, span] = nn(v_turned[:, 0:length], part.astype(BF16)).astype(BF16)

    def backward(head):
        columns = slice(head * 128, head * 128 + 128)
        for span, length in spans():
            grad = grad_att[span, columns]
            part = probs[head, 0:length, span]
            dprobs = nt(v_full[0:length], grad)
            delta = jnp.sum(part * dprobs, axis=0, keepdims=True)
            dscores = (part * (dprobs - delta) * scale).astype(BF16)
            gq_ref[span, columns] = nn(k_turned[:, 0:length], dscores).T.astype(BF16)
            key_part = nn(dscores, q_ref[span, columns])
            value_part = nn(part.astype(BF16), grad)
            if head == 0 and length == 256:
                key_acc[256:512] = jnp.zeros((256, 128), F32)
                value_acc[256:512] = jnp.zeros((256, 128), F32)
                key_acc[0:256] = key_part
                value_acc[0:256] = value_part
            else:
                key_acc[0:length] += key_part
                value_acc[0:length] += value_part

    def parts_send():
        key, value = key_acc[...].astype(BF16), value_acc[...].astype(BF16)
        low = jnp.concatenate([key[:, 0:64], value[:, 0:64]], 1)
        high = jnp.concatenate([key[:, 64:128], value[:, 64:128]], 1)
        part_send[...] = jnp.where(parity == 0, high, low)
        copies.pop("kv").wait_send()
        kv_send[...] = jnp.where(parity == 0, low, high)
        send("parts", part_send, part_recv, to_partner)

    def parts_done():
        arrived("parts")
        both = (kv_send[...].astype(F32) + part_recv[...].astype(F32)).astype(BF16)
        gk_ref[...] = both[:, 0:64]
        gv_ref[...] = both[:, 64:128]

    def gather_term(place):
        arrived(("wc", place))
        for half in range(2):
            columns = slice(half * 256, half * 256 + 256)
            product = nn(
                gbuf[place].reshape(512, 512), wbuf[place, :, :, columns].reshape(512, 256)
            )
            if place == 0:
                total[:, columns] = product
            else:
                total[:, columns] += product
            if place == 7:
                grad_att[:, columns] = total[:, columns].astype(BF16)

    def weight_term(place):
        features = gbuf[place].reshape(512, 512)
        product = nn(att[...], features[:, 0:256])
        core_send[place, 0] = product[:, 0:128].astype(BF16)
        core_send[place, 1] = product[:, 128:256].astype(BF16)
        send(("core", place), core_send.at[place], core_recv.at[place], to_core)
        terms[place] = nn(att[...], features[:, 256:512])

    def ring(place):
        relative = ORDER[place]
        arrived(("core", place))
        if relative != 4:
            if relative >= 0:
                arrived(("ring", relative + 1, True))
            if relative <= 0:
                arrived(("ring", relative - 1, False))
        for at in range(2):
            partial = terms[place, :, at * 128 : at * 128 + 128] + core_recv[place, at].astype(F32)
            if relative == 3 and at == 0 or relative == -3 and at == 1 or 0 < abs(relative) < 3:
                partial += y_recv[place, at].astype(F32)
            if relative == 0:
                partial += y_recv[place, at].astype(F32) + y_recv[ABOVE, at].astype(F32)
                terms[place, :, at * 128 : at * 128 + 128] = partial
            else:
                y_send[place, at] = partial.astype(BF16)
        if relative == 4:
            send(("ring", 4, True), y_send.at[place, 0], y_recv.at[AT[3], 0], to_y_up)
            send(("ring", -4, False), y_send.at[place, 1], y_recv.at[AT[-3], 1], to_y_down)
        elif relative > 0:
            send(("ring", relative, True), y_send.at[place], y_recv.at[AT[relative - 1]], to_y_up)
        elif relative < 0:
            slot = ABOVE if relative == -1 else AT[relative + 1]
            send(("ring", relative, False), y_send.at[place], y_recv.at[slot], to_y_down)
        else:
            low, high = terms[place, :, 0:128], terms[place, :, 128:256]
            z_send[...] = jnp.where(zl == 0, high, low).astype(BF16)
            send("pair", z_send, z_recv, to_pair)

    def ring_done():
        arrived("pair")
        low, high = terms[AT[0], :, 0:128], terms[AT[0], :, 128:256]
        final = jnp.where(zl == 0, low, high) + z_recv[...].astype(F32)
        gw_ref[...] = final.T.astype(BF16)

    send("kv", kv_send, kv_recv, to_partner)
    w_start()
    g_z1(0)
    g_z1(1)
    g_z1(2)
    g_z2(0)
    g_x1(0)
    w_pair()
    g_z2(1)
    g_z1(3)
    kv_ready()
    g_x1(1)
    forward(0)
    w_next("a", 1)
    g_x2(0)
    forward(1)
    g_z2(2)
    g_z1(4)
    g_x1(2)
    w_next("b", 1)
    forward(2)
    g_x2(1)
    w_next("a", 2)
    forward(3)
    g_z2(3)
    g_z1(5)
    g_done(0)
    weight_term(0)
    g_x1(3)
    w_next("b", 2)
    ring(0)
    g_x2(2)
    w_next("a", 3)
    g_z2(4)
    g_z1(6)
    g_done(1)
    weight_term(1)
    g_x1(4)
    w_next("b", 3)
    g_x2(3)
    ring(1)
    g_done(2)
    weight_term(2)
    g_z2(5)
    g_z1(7)
    g_x1(5)
    w_last()
    ring(2)
    g_x2(4)
    gather_term(0)
    gather_term(1)
    gather_term(2)
    g_done(3)
    weight_term(3)
    g_z2(6)
    g_x1(6)
    g_x2(5)
    gather_term(3)
    ring(3)
    g_done(4)
    weight_term(4)
    g_z2(7)
    g_x1(7)
    g_x2(6)
    gather_term(4)
    ring(4)
    g_done(5)
    weight_term(5)
    gather_term(5)
    g_x2(7)
    ring(5)
    g_done(6)
    weight_term(6)
    gather_term(6)
    ring(6)
    g_done(7)
    weight_term(7)
    gather_term(7)
    backward(0)
    ring(7)
    backward(1)
    backward(2)
    backward(3)
    parts_send()
    ring_done()
    parts_done()
    for copy in copies.values():
        copy.wait_send()


def body(queries, keys, values, grad_out, out_weight):
    vmem = pl.BlockSpec(memory_space=pltpu.VMEM)
    return pl.pallas_call(
        kernel,
        out_shape=(
            jax.ShapeDtypeStruct((512, 512), BF16),
            jax.ShapeDtypeStruct((512, 64), BF16),
            jax.ShapeDtypeStruct((512, 64), BF16),
            jax.ShapeDtypeStruct((128, 512), BF16),
        ),
        in_specs=[vmem] * 5,
        out_specs=(vmem,) * 4,
        scratch_shapes=[
            pltpu.VMEM((8, 4, 128, 512), BF16),
            pltpu.VMEM((8, 4, 128, 512), BF16),
            pltpu.VMEM((512, 128), BF16),
            pltpu.VMEM((512, 128), BF16),
            pltpu.VMEM((512, 128), BF16),
            pltpu.VMEM((512, 128), BF16),
            pltpu.VMEM((128, 512), BF16),
            pltpu.VMEM((128, 512), BF16),
            pltpu.VMEM((4, 512, 512), F32),
            pltpu.VMEM((512, 512), BF16),
            pltpu.VMEM((512, 512), F32),
            pltpu.VMEM((512, 512), BF16),
            pltpu.VMEM((8, 512, 256), F32),
            pltpu.VMEM((8, 2, 512, 128), BF16),
            pltpu.VMEM((8, 2, 512, 128), BF16),
            pltpu.VMEM((8, 2, 512, 128), BF16),
            pltpu.VMEM((9, 2, 512, 128), BF16),
            pltpu.VMEM((512, 128), BF16),
            pltpu.VMEM((512, 128), BF16),
            pltpu.VMEM((512, 128), F32),
            pltpu.VMEM((512, 128), F32),
            pltpu.VMEM((512, 128), BF16),
            pltpu.VMEM((512, 128), BF16),
            pltpu.SemaphoreType.DMA((N_COPIES,)),
            pltpu.SemaphoreType.DMA((N_COPIES,)),
        ],
        compiler_params=pltpu.CompilerParams(
            collective_id=0, has_side_effects=True, vmem_limit_bytes=56 * 1024 * 1024
        ),
        cost_estimate=pl.CostEstimate(
            flops=6_000_000_000, bytes_accessed=4_000_000, transcendentals=1_000_000
        ),
    )(queries, keys, values, grad_out, out_weight)


def solution(mesh):
    placed = (
        P("dp", "tensor"),
        P("dp", "tensor"),
        P("dp", "tensor"),
        P(("dp", "tensor"), None),
        P("dp", "tensor"),
    )
    return jax.shard_map(
        body,
        mesh=mesh,
        in_specs=placed,
        out_specs=(P("dp", "tensor"), P("dp", "tensor"), P("dp", "tensor"), P("dp", "tensor")),
        check_vma=False,
    )
```

```python
import jax
import jax.numpy as jnp
from jax import lax
from jax.experimental import pallas as pl
from jax.experimental.pallas import tpu as pltpu
from jax.sharding import PartitionSpec as P

HEAD_DIM = 128
MESH = pl.DeviceIdType.MESH
F32 = jnp.float32
BF16 = jnp.bfloat16

ORDER = (4, 3, -3, 2, -2, 1, -1, 0)
AT = {relative: place for place, relative in enumerate(ORDER)}
AT[-4] = AT[4]
ABOVE = 8

NX, NZ, NY = 4, 4, 8
N_COPIES = 208

WAY = tuple('PPPPPPZZ')


def nt(a, b):
    return lax.dot_general(a, b, (((1,), (1,)), ((), ())), preferred_element_type=F32)


def nn(a, b):
    return lax.dot_general(a, b, (((1,), (0,)), ((), ())), preferred_element_type=F32)


def kernel(
    q_ref, k_ref, v_ref, g_ref, w_ref,
    gq_ref, gk_ref, gv_ref, gw_ref,
    gbuf, wbuf, kv_send, kv_recv, k_full, v_full, k_turned, v_turned,
    probs, att, total, grad_att, terms, core_send, core_recv, y_send, y_recv,
    z_send, z_recv, key_acc, value_acc, key_part, value_part, key_recv, value_recv, send_sem, recv_sem,
):
    scale = HEAD_DIM ** (-0.5)
    dp = lax.axis_index("dp")
    tensor = lax.axis_index("tensor")
    core = lax.rem(dp, 2)
    y = lax.rem(dp // 2, NY)
    zl = dp // (2 * NY)
    x = tensor // NZ
    zh = lax.rem(tensor, NZ)
    parity = lax.rem(tensor, 2)

    def device(core=core, y=y, zl=zl, x=x, zh=zh):
        return ((zl * NY + y) * 2 + core, x * NZ + zh)

    x_up, x_down = lax.rem(x + 1, NX), lax.rem(x + NX - 1, NX)
    z_up, z_down = lax.rem(zh + 1, NZ), lax.rem(zh + NZ - 1, NZ)
    to_x_up, to_x_down = device(x=x_up), device(x=x_down)
    to_z_up, to_z_down = device(zh=z_up), device(zh=z_down)
    to_y_up = device(y=lax.rem(y + 1, NY))
    to_y_down = device(y=lax.rem(y + NY - 1, NY))
    to_pair = device(zl=1 - zl)
    to_core = device(core=1 - core)
    to_partner = (dp, tensor + 1 - 2 * parity)

    barrier = pltpu.get_barrier_semaphore()
    for target in (to_x_up, to_x_down, to_z_up, to_z_down, to_y_up, to_y_down, to_pair, to_core):
        pl.semaphore_signal(barrier, inc=1, device_id=target, device_id_type=MESH)

    copies = {}

    def send(name, source, target, to):
        index = len(copies)
        copy = pltpu.make_async_remote_copy(
            src_ref=source, dst_ref=target, send_sem=send_sem.at[index], recv_sem=recv_sem.at[index],
            device_id=to, device_id_type=MESH,
        )
        copy.start()
        copies[name] = copy

    waited = set()

    def arrived(*names):
        for name in names:
            if name not in waited:
                copies[name].wait_recv()
                waited.add(name)

    kv_send[0:64] = k_ref[...]
    kv_send[64:128] = v_ref[...]
    wbuf[AT[0], 2 + zl] = w_ref[...]
    own_rows = pl.ds(pl.multiple_of(zh * 32, 32), 32)
    for place, relative in enumerate(ORDER):
        column = lax.rem(y + relative + NY, NY)
        for slot in range(4):
            of_core = core if slot >= 2 else 1 - core
            block = ((slot % 2) * NY + column) * 2 + of_core
            gbuf[place, x, own_rows, slot * 128 : (slot + 1) * 128] = g_ref[
                :, pl.ds(pl.multiple_of(block * 128, 128), 128)
            ]
    pl.semaphore_wait(barrier, 8)

    def z_rows(at, first, count):
        return pl.ds(pl.multiple_of(at * 32 + first, 16), count)

    to_x, to_y, to_z = (
        {"u": to_x_up, "d": to_x_down}, {"u": to_y_up, "d": to_y_down}, {"u": to_z_up, "d": to_z_down},
    )
    from_x, from_z = {"u": x_down, "d": x_up}, {"u": z_down, "d": z_up}
    kept = {"u": 0, "d": 16}
    pieces = {"own": zh, "down": z_down, "up": z_up, "far": lax.rem(zh + 2, NZ)}
    before = {"own": (), "down": ("u",), "up": ("d",), "far": ("u", "d")}

    def g_z1(place, way):
        if WAY[place] == "X":
            arrived(("x2", place, "u", None), ("x2", place, "d", None))
            block = gbuf.at[place, :, z_rows(zh, 0, 32)]
        else:
            block = gbuf.at[place, x, z_rows(zh, 0, 32)]
        send(("z1", place, way), block, block, to_z[way])

    def g_z2(place, way):
        arrived(("z1", place, way))
        rows = z_rows(from_z[way], kept[way], 16)
        block = gbuf.at[place, :, rows] if WAY[place] == "X" else gbuf.at[place, x, rows]
        send(("z2", place, way), block, block, to_z[way])

    def g_x1(place, way, piece=None):
        if WAY[place] == "X":
            block = gbuf.at[place, x, z_rows(zh, 0, 32)]
        elif piece is None:
            arrived(("z2", place, "u"), ("z2", place, "d"))
            block = gbuf.at[place, x]
        else:
            kind = "z2" if piece == "far" else "z1"
            arrived(*((kind, place, which) for which in before[piece]))
            block = gbuf.at[place, x, z_rows(pieces[piece], 0, 32)]
        send(("x1", place, way, piece), block, block, to_x[way])

    def g_x2(place, way, piece=None):
        arrived(("x1", place, way, piece))
        if WAY[place] == "X":
            rows = z_rows(zh, kept[way], 16)
        elif piece is None:
            rows = pl.ds(kept[way] * 4, 64)
        else:
            rows = z_rows(pieces[piece], kept[way], 16)
        block = gbuf.at[place, from_x[way], rows]
        send(("x2", place, way, piece), block, block, to_x[way])

    def g_done(place):
        for way in ("u", "d"):
            if WAY[place] == "X":
                arrived(("z2", place, way))
            elif WAY[place] == "P":
                arrived(*(("x2", place, way, piece) for piece in pieces))
            else:
                arrived(("x2", place, way, None))

    row = {"a": 2 + zl, "b": 3 - zl}

    def w_hop(block, step, way):
        if step > 1:
            arrived(("w", block, step - 1, way))
        elif block == "b":
            arrived("wz")
        relative = (1 - step) if way == "u" else (step - 1)
        source = wbuf.at[AT[relative], row[block]]
        target = wbuf.at[AT[relative - 1 if way == "u" else relative + 1], row[block]]
        send(("w", block, step, way), source, target, to_y[way])

    def w_pair():
        own = wbuf.at[AT[0], row["a"]]
        send("wz", own, own, to_pair)

    def w_core(relative):
        if relative == 0:
            arrived("wz")
        elif relative == 4:
            arrived(("w", "a", 4, "u"), ("w", "b", 4, "d"))
        else:
            way = "d" if relative > 0 else "u"
            arrived(("w", "a", abs(relative), way), ("w", "b", abs(relative), way))
        place = AT[relative]
        send(("wc", place), wbuf.at[place, 2:4], wbuf.at[place, 0:2], to_core)

    spans = (slice(0, 256), slice(256, 512))
    mine = pl.ds(pl.multiple_of(parity * 64, 64), 64)
    other = pl.ds(pl.multiple_of(64 - parity * 64, 64), 64)

    def kv_start():
        send("kv", kv_send, kv_recv, to_partner)

    def kv_ready():
        arrived("kv")
        k_turned[mine] = kv_send[0:64]
        v_turned[mine] = kv_send[64:128]
        k_turned[other] = kv_recv[0:64]
        v_turned[other] = kv_recv[64:128]
        k_full[...] = k_turned[...].astype(F32).T.astype(BF16)
        v_full[...] = v_turned[...].astype(F32).T.astype(BF16)

    def forward(head):
        columns = slice(head * 128, head * 128 + 128)
        for span in spans:
            length = span.stop
            scores = nt(k_full[0:length], q_ref[span, columns]) * scale
            key_at = lax.broadcasted_iota(jnp.int32, (length, 256), 0)
            query_at = lax.broadcasted_iota(jnp.int32, (length, 256), 1) + span.start
            scores = jnp.where(key_at <= query_at, scores, -jnp.inf)
            powers = jnp.exp(scores - jnp.max(scores, axis=0, keepdims=True))
            part = powers * (1.0 / jnp.sum(powers, axis=0, keepdims=True))
            probs[head, 0:length, span] = part
            att[columns, span] = nn(v_turned[:, 0:length], part.astype(BF16)).astype(BF16)

    def backward_values():
        for head in range(4):
            columns = slice(head * 128, head * 128 + 128)
            for span in spans[::-1]:
                length = span.stop
                part = nn(probs[head, 0:length, span].astype(BF16), grad_att[span, columns])
                if head == 0 and length == 512:
                    value_acc[...] = part
                else:
                    value_acc[0:length] += part
        value_part[...] = value_acc[...].T.astype(BF16)

    def backward_keys(at):
        span = spans[at]
        length = span.stop
        for head in range(4):
            columns = slice(head * 128, head * 128 + 128)
            part = probs[head, 0:length, span]
            dprobs = nt(v_full[0:length], grad_att[span, columns])
            delta = jnp.sum(part * dprobs, axis=0, keepdims=True)
            dscores = (part * (dprobs - delta) * scale).astype(BF16)
            gq_ref[span, columns] = nn(k_turned[:, 0:length], dscores).T.astype(BF16)
            product = nn(dscores, q_ref[span, columns])
            if head == 0 and at == 1:
                key_acc[...] = product
            else:
                key_acc[0:length] += product
        key_part[:, span] = key_acc[span].T.astype(BF16)

    def part_start(which):
        if which == 0:
            send(("part", 0), value_part.at[other], value_recv, to_partner)
        else:
            span = spans[2 - which]
            send(("part", which), key_part.at[other, span], key_recv.at[:, span], to_partner)

    def parts_done():
        arrived(("part", 0), ("part", 1), ("part", 2))
        gk_ref[...] = (key_part[mine].astype(F32) + key_recv[...].astype(F32)).astype(BF16)
        gv_ref[...] = (value_part[mine].astype(F32) + value_recv[...].astype(F32)).astype(BF16)

    summed = []

    def gather_term(place):
        g_done(place)
        arrived(("wc", place))
        for half in range(2):
            columns = slice(half * 256, half * 256 + 256)
            product = nn(
                gbuf[place].reshape(512, 512), wbuf[place, :, :, columns].reshape(512, 256)
            )
            if not summed:
                total[:, columns] = product
            elif len(summed) < 7:
                total[:, columns] += product
            else:
                grad_att[:, columns] = (total[:, columns] + product).astype(BF16)
        summed.append(place)

    def weight_term(place):
        g_done(place)
        features = gbuf[place].reshape(512, 512)
        product = nn(att[...], features[:, 0:256])
        core_send[place, 0] = product[:, 0:128].astype(BF16)
        core_send[place, 1] = product[:, 128:256].astype(BF16)

    def core_start(place):
        send(("core", place), core_send.at[place], core_recv.at[place], to_core)
        features = gbuf[place].reshape(512, 512)
        product = nn(att[...], features[:, 256:512])
        terms[place, 0] = product[:, 0:128]
        terms[place, 1] = product[:, 128:256]

    at_of = {"a": zl, "b": 1 - zl}

    def ring(block, place):
        relative = ORDER[place]
        at = at_of[block]
        arrived(("core", place))
        partial = terms[place, at] + core_recv[place, at].astype(F32)
        if relative != 4 and (relative, block) not in ((3, "b"), (-3, "a")):
            if relative >= 0:
                arrived(("ring", block, relative + 1, "u"))
                partial += y_recv[place, at].astype(F32)
            if relative <= 0:
                arrived(("ring", block, relative - 1, "d"))
                slot = ABOVE if relative == 0 else place
                partial += y_recv[slot, at].astype(F32)
        if relative:
            y_send[place, at] = partial.astype(BF16)
        elif block == "b":
            z_send[...] = partial.astype(BF16)
        else:
            terms[place, at] = partial

    def ring_start(block, place):
        relative = ORDER[place]
        at = at_of[block]
        up = block == "a" if relative == 4 else relative > 0
        if up:
            relative, slot, way = relative, AT[relative - 1], "u"
        else:
            relative = -abs(relative)
            slot, way = ABOVE if relative == -1 else AT[relative + 1], "d"
        send(("ring", block, relative, way), y_send.at[place, at], y_recv.at[slot, at], to_y[way])

    def pair_start():
        send("pair", z_send, z_recv, to_pair)

    def ring_done():
        arrived("pair")
        gw_ref[...] = (terms[AT[0], zl] + z_recv[...].astype(F32)).T.astype(BF16)

    g_x1(0, "d", "own")
    g_x1(0, "u", "own")
    g_x1(1, "d", "own")
    g_x1(1, "u", "own")
    g_z1(0, "d")
    g_z1(0, "u")
    g_z1(1, "d")
    g_z1(1, "u")
    w_hop("a", 1, "d")
    w_hop("a", 1, "u")
    g_x1(2, "d", "own")
    g_x1(2, "u", "own")
    g_x1(3, "d", "own")
    g_x1(3, "u", "own")
    g_z1(2, "d")
    w_pair()
    g_x1(4, "d", "own")
    g_x1(4, "u", "own")
    g_x1(5, "d", "own")
    g_x1(5, "u", "own")
    g_z1(3, "d")
    g_z1(2, "u")
    g_x2(0, "d", "own")
    g_x2(0, "u", "own")
    g_x2(1, "d", "own")
    g_x2(1, "u", "own")
    g_z1(4, "d")
    g_x2(2, "d", "own")
    g_x2(2, "u", "own")
    g_x2(3, "d", "own")
    g_x2(3, "u", "own")
    w_hop("a", 2, "d")
    g_x1(0, "d", "up")
    g_x1(0, "u", "down")
    w_hop("a", 2, "u")
    g_x1(0, "d", "down")
    g_x1(0, "u", "up")
    g_z2(0, "d")
    g_z2(0, "u")
    g_x2(4, "d", "own")
    g_x2(4, "u", "own")
    g_x1(1, "d", "down")
    g_x1(1, "u", "down")
    g_x1(1, "d", "up")
    g_x1(1, "u", "up")
    g_z2(1, "d")
    g_z2(1, "u")
    g_x2(5, "d", "own")
    g_x2(5, "u", "own")
    g_z1(5, "d")
    g_z1(3, "u")
    g_x1(2, "d", "up")
    g_x1(2, "u", "up")
    g_z2(2, "d")
    g_z1(4, "u")
    g_x2(0, "d", "up")
    g_x2(0, "u", "down")
    g_x2(0, "d", "down")
    g_x2(0, "u", "up")
    w_hop("b", 1, "d")
    w_hop("b", 1, "u")
    g_x1(3, "d", "up")
    g_x1(3, "u", "up")
    w_core(0)
    g_z2(3, "d")
    kv_start()
    w_hop("a", 3, "d")
    w_hop("a", 3, "u")
    g_x2(1, "d", "down")
    g_x2(1, "u", "down")
    g_z1(6, "d")
    g_x1(4, "d", "up")
    g_x1(2, "d", "down")
    g_x1(2, "u", "down")
    g_x1(4, "u", "up")
    g_z2(4, "d")
    g_z2(2, "u")
    g_x2(1, "d", "up")
    g_x2(1, "u", "up")
    g_x1(0, "d", "far")
    g_x1(0, "u", "far")
    g_x1(1, "d", "far")
    g_x1(1, "u", "far")
    g_z1(7, "d")
    g_x2(2, "d", "up")
    g_x2(2, "u", "up")
    g_z2(5, "d")
    g_x2(3, "d", "up")
    g_x2(3, "u", "up")
    g_x1(3, "d", "down")
    g_x1(3, "u", "down")
    g_z2(3, "u")
    g_x2(4, "d", "up")
    g_x2(2, "u", "down")
    w_hop("b", 2, "d")
    w_hop("b", 2, "u")
    w_core(1)
    w_core(-1)
    g_z1(5, "u")
    g_x2(2, "d", "down")
    g_x2(4, "u", "up")
    g_x1(4, "d", "down")
    g_x1(4, "u", "down")
    g_x1(5, "d", "up")
    g_x1(5, "u", "up")
    g_z2(4, "u")
    g_x2(0, "d", "far")
    g_x2(0, "u", "far")
    g_z2(6, "d")
    g_x2(1, "d", "far")
    g_x2(1, "u", "far")
    w_hop("a", 4, "u")
    g_z1(6, "u")
    g_x2(3, "d", "down")
    g_x2(3, "u", "down")
    g_z1(7, "u")
    kv_ready()
    forward(0)
    g_z2(7, "d")
    g_x1(2, "d", "far")
    g_x1(2, "u", "far")
    forward(1)
    g_x2(4, "d", "down")
    g_x2(4, "u", "down")
    forward(2)
    g_x1(3, "d", "far")
    g_x1(3, "u", "far")
    w_hop("b", 3, "d")
    w_hop("b", 3, "u")
    g_x2(5, "d", "up")
    g_x2(5, "u", "up")
    w_core(2)
    w_core(-2)
    forward(3)
    weight_term(0)
    core_start(0)
    g_z2(5, "u")
    g_x1(5, "d", "down")
    g_x1(5, "u", "down")
    weight_term(1)
    core_start(1)
    g_x1(4, "d", "far")
    g_x1(4, "u", "far")
    g_x2(2, "d", "far")
    g_x2(2, "u", "far")
    g_z2(6, "u")
    g_x2(3, "d", "far")
    g_x2(3, "u", "far")
    ring("a", 0)
    ring_start("a", 0)
    ring("b", 0)
    ring_start("b", 0)
    ring("b", 1)
    ring_start("b", 1)
    g_z2(7, "u")
    g_x2(5, "d", "down")
    g_x2(5, "u", "down")
    w_hop("b", 4, "d")
    w_core(3)
    w_core(-3)
    g_x2(4, "d", "far")
    g_x2(4, "u", "far")
    weight_term(2)
    core_start(2)
    g_x1(5, "d", "far")
    g_x1(5, "u", "far")
    weight_term(3)
    core_start(3)
    gather_term(1)
    gather_term(3)
    g_x1(6, "d")
    g_x1(6, "u")
    gather_term(2)
    weight_term(4)
    core_start(4)
    ring("a", 2)
    ring_start("a", 2)
    ring("a", 1)
    ring_start("a", 1)
    ring("b", 2)
    g_x1(7, "d")
    g_x1(7, "u")
    ring_start("b", 2)
    gather_term(4)
    g_x2(5, "d", "far")
    g_x2(5, "u", "far")
    ring("b", 3)
    ring_start("b", 3)
    w_core(4)
    g_x2(6, "d")
    g_x2(6, "u")
    gather_term(0)
    ring("a", 4)
    ring_start("a", 4)
    ring("a", 3)
    ring_start("a", 3)
    g_x2(7, "d")
    g_x2(7, "u")
    weight_term(5)
    core_start(5)
    gather_term(5)
    ring("b", 4)
    ring_start("b", 4)
    weight_term(6)
    core_start(6)
    gather_term(6)
    ring("b", 5)
    ring_start("b", 5)
    ring("a", 6)
    ring_start("a", 6)
    ring("a", 5)
    ring_start("a", 5)
    gather_term(7)
    weight_term(7)
    core_start(7)
    backward_values()
    part_start(0)
    backward_keys(1)
    part_start(1)
    ring("b", 6)
    ring_start("b", 6)
    backward_keys(0)
    part_start(2)
    ring("a", 7)
    ring("b", 7)
    pair_start()
    parts_done()
    ring_done()
    for copy in copies.values():
        copy.wait_send()


def body(queries, keys, values, grad_out, out_weight):
    vmem = pl.BlockSpec(memory_space=pltpu.VMEM)
    grad_q, grad_k, grad_v, grad_weight = pl.pallas_call(
        kernel,
        out_shape=(
            jax.ShapeDtypeStruct((512, 512), BF16),
            jax.ShapeDtypeStruct((64, 512), BF16),
            jax.ShapeDtypeStruct((64, 512), BF16),
            jax.ShapeDtypeStruct((128, 512), BF16),
        ),
        in_specs=[vmem] * 5,
        out_specs=(vmem,) * 4,
        scratch_shapes=[
            pltpu.VMEM((8, 4, 128, 512), BF16),
            pltpu.VMEM((8, 4, 128, 512), BF16),
            pltpu.VMEM((128, 512), BF16),
            pltpu.VMEM((128, 512), BF16),
            pltpu.VMEM((512, 128), BF16),
            pltpu.VMEM((512, 128), BF16),
            pltpu.VMEM((128, 512), BF16),
            pltpu.VMEM((128, 512), BF16),
            pltpu.VMEM((4, 512, 512), F32),
            pltpu.VMEM((512, 512), BF16),
            pltpu.VMEM((512, 512), F32),
            pltpu.VMEM((512, 512), BF16),
            pltpu.VMEM((8, 2, 512, 128), F32),
            pltpu.VMEM((8, 2, 512, 128), BF16),
            pltpu.VMEM((8, 2, 512, 128), BF16),
            pltpu.VMEM((8, 2, 512, 128), BF16),
            pltpu.VMEM((9, 2, 512, 128), BF16),
            pltpu.VMEM((512, 128), BF16),
            pltpu.VMEM((512, 128), BF16),
            pltpu.VMEM((512, 128), F32),
            pltpu.VMEM((512, 128), F32),
            pltpu.VMEM((128, 512), BF16),
            pltpu.VMEM((128, 512), BF16),
            pltpu.VMEM((64, 512), BF16),
            pltpu.VMEM((64, 512), BF16),
            pltpu.SemaphoreType.DMA((N_COPIES,)),
            pltpu.SemaphoreType.DMA((N_COPIES,)),
        ],
        compiler_params=pltpu.CompilerParams(
            collective_id=0, has_side_effects=True, vmem_limit_bytes=56 * 1024 * 1024
        ),
        cost_estimate=pl.CostEstimate(
            flops=6_000_000_000, bytes_accessed=4_000_000, transcendentals=1_000_000
        ),
    )(queries, keys.T, values.T, grad_out, out_weight)
    return grad_q, grad_k.T, grad_v.T, grad_weight


def solution(mesh):
    placed = (
        P("dp", "tensor"),
        P("dp", "tensor"),
        P("dp", "tensor"),
        P(("dp", "tensor"), None),
        P("dp", "tensor"),
    )
    return jax.shard_map(
        body,
        mesh=mesh,
        in_specs=placed,
        out_specs=(P("dp", "tensor"), P("dp", "tensor"), P("dp", "tensor"), P("dp", "tensor")),
        check_vma=False,
    )
```

```python
import jax
import jax.numpy as jnp
from jax import lax
from jax.experimental import pallas as pl
from jax.experimental.pallas import tpu as pltpu
from jax.sharding import PartitionSpec as P

HEAD_DIM = 128
MESH = pl.DeviceIdType.MESH
F32 = jnp.float32
BF16 = jnp.bfloat16

ORDER = (4, 3, -3, 2, -2, 1, -1, 0)
AT = {relative: place for place, relative in enumerate(ORDER)}
AT[-4] = AT[4]
ABOVE = 8

NX, NZ, NY = 4, 4, 8
N_COPIES = 224

PAIR, W_PAIR = 4, 5

WAY = tuple('PPPPPPZZ')


def nt(a, b):
    return lax.dot_general(a, b, (((1,), (1,)), ((), ())), preferred_element_type=F32)


def nn(a, b):
    return lax.dot_general(a, b, (((1,), (0,)), ((), ())), preferred_element_type=F32)


def kernel(
    q_in, k_in, v_in, g_in, w_in,
    gq_out, gk_out, gv_out, gw_out,
    q_ref, g_ref, gq_ref, gk_ref, gv_ref, gw_ref, local_sem,
    gbuf, wbuf, kv_send, kv_recv, k_full, v_full, k_turned, v_turned,
    probs, att, total, grad_att, terms, core_send, core_recv, y_send, y_recv,
    z_send, z_recv, key_acc, value_acc, key_part, value_part, key_recv, value_recv, send_sem, recv_sem,
):
    scale = HEAD_DIM ** (-0.5)
    dp = lax.axis_index("dp")
    tensor = lax.axis_index("tensor")
    core = lax.rem(dp, 2)
    y = lax.rem(dp // 2, NY)
    zl = dp // (2 * NY)
    x = tensor // NZ
    zh = lax.rem(tensor, NZ)
    parity = lax.rem(tensor, 2)

    def device(core=core, y=y, zl=zl, x=x, zh=zh):
        return ((zl * NY + y) * 2 + core, x * NZ + zh)

    x_up, x_down = lax.rem(x + 1, NX), lax.rem(x + NX - 1, NX)
    z_up, z_down = lax.rem(zh + 1, NZ), lax.rem(zh + NZ - 1, NZ)
    to_x_up, to_x_down = device(x=x_up), device(x=x_down)
    to_z_up, to_z_down = device(zh=z_up), device(zh=z_down)
    to_y_up = device(y=lax.rem(y + 1, NY))
    to_y_down = device(y=lax.rem(y + NY - 1, NY))
    to_pair = device(zl=1 - zl)
    to_core = device(core=1 - core)
    to_partner = (dp, tensor + 1 - 2 * parity)

    barrier = pltpu.get_barrier_semaphore()
    for target in (to_x_up, to_x_down, to_z_up, to_z_down, to_y_up, to_y_down, to_pair, to_core):
        pl.semaphore_signal(barrier, inc=1, device_id=target, device_id_type=MESH)

    copies = {}

    def send(name, source, target, to):
        index = len(copies)
        copy = pltpu.make_async_remote_copy(
            src_ref=source, dst_ref=target, send_sem=send_sem.at[index], recv_sem=recv_sem.at[index],
            device_id=to, device_id_type=MESH,
        )
        copy.start()
        copies[name] = copy

    waited = set()

    def arrived(*names):
        for name in names:
            if name not in waited:
                copies[name].wait_recv()
                waited.add(name)

    loads = [
        pltpu.make_async_copy(source, target, local_sem.at[i])
        for i, (source, target) in enumerate((
            (g_in, g_ref), (k_in, kv_send.at[0:64]), (v_in, kv_send.at[64:128]),
            (w_in, wbuf.at[AT[0], 2 + zl]), (q_in, q_ref),
        ))
    ]
    for load in loads:
        load.start()
    stores = []

    def store(source, target):
        copy = pltpu.make_async_copy(source, target, local_sem.at[len(loads) + len(stores)])
        copy.start()
        stores.append(copy)

    loads[0].wait()
    own_rows = pl.ds(pl.multiple_of(zh * 32, 32), 32)
    for place, relative in enumerate(ORDER):
        column = lax.rem(y + relative + NY, NY)
        for slot in range(4):
            of_core = core if slot >= 2 else 1 - core
            block = ((slot % 2) * NY + column) * 2 + of_core
            gbuf[place, x, own_rows, slot * 128 : (slot + 1) * 128] = g_ref[
                :, pl.ds(pl.multiple_of(block * 128, 128), 128)
            ]
    for load in loads[1:4]:
        load.wait()
    pl.semaphore_wait(barrier, 8)

    def z_rows(at, first, count):
        return pl.ds(pl.multiple_of(at * 32 + first, 16), count)

    to_x, to_y, to_z = (
        {"u": to_x_up, "d": to_x_down}, {"u": to_y_up, "d": to_y_down}, {"u": to_z_up, "d": to_z_down},
    )
    from_x, from_z = {"u": x_down, "d": x_up}, {"u": z_down, "d": z_up}
    kept = {"u": 0, "d": 16}
    pieces = {"own": zh, "down": z_down, "up": z_up, "far": lax.rem(zh + 2, NZ)}
    before = {"own": (), "down": ("u",), "up": ("d",), "far": ("u", "d")}

    def g_z1(place, way):
        if WAY[place] == "X":
            arrived(("x2", place, "u", None), ("x2", place, "d", None))
            block = gbuf.at[place, :, z_rows(zh, 0, 32)]
        else:
            block = gbuf.at[place, x, z_rows(zh, 0, 32)]
        send(("z1", place, way), block, block, to_z[way])

    def g_z2(place, way):
        arrived(("z1", place, way))
        rows = z_rows(from_z[way], kept[way], 16)
        block = gbuf.at[place, :, rows] if WAY[place] == "X" else gbuf.at[place, x, rows]
        send(("z2", place, way), block, block, to_z[way])

    def g_x1(place, way, piece=None):
        if WAY[place] == "X":
            block = gbuf.at[place, x, z_rows(zh, 0, 32)]
        elif piece is None:
            arrived(("z2", place, "u"), ("z2", place, "d"))
            block = gbuf.at[place, x]
        else:
            kind = "z2" if piece == "far" else "z1"
            arrived(*((kind, place, which) for which in before[piece]))
            block = gbuf.at[place, x, z_rows(pieces[piece], 0, 32)]
        send(("x1", place, way, piece), block, block, to_x[way])

    def g_x2(place, way, piece=None):
        arrived(("x1", place, way, piece))
        if WAY[place] == "X":
            rows = z_rows(zh, kept[way], 16)
        elif piece is None:
            rows = pl.ds(kept[way] * 4, 64)
        else:
            rows = z_rows(pieces[piece], kept[way], 16)
        block = gbuf.at[place, from_x[way], rows]
        send(("x2", place, way, piece), block, block, to_x[way])

    def g_done(place):
        for way in ("u", "d"):
            if WAY[place] == "X":
                arrived(("z2", place, way))
            elif WAY[place] == "P":
                arrived(*(("x2", place, way, piece) for piece in pieces))
            else:
                arrived(("x2", place, way, None))

    row = {"a": 2 + zl, "b": 3 - zl}

    def w_hop(block, step, way):
        if step > 1:
            arrived(("w", block, step - 1, way))
        elif block == "b":
            arrived(("wz", AT[0]))
        relative = (1 - step) if way == "u" else (step - 1)
        source = wbuf.at[AT[relative], row[block]]
        target = wbuf.at[AT[relative - 1 if way == "u" else relative + 1], row[block]]
        if step == 4 and W_PAIR <= 4:
            rows = slice(0, 64) if way == "u" else slice(64, 128)
            source, target = source.at[rows], target.at[rows]
        send(("w", block, step, way), source, target, to_y[way])

    def w_arrived(block, relative):
        far = abs(relative)
        if block == "b" and (relative == 0 or far >= W_PAIR):
            arrived(("wz", AT[relative]))
        elif far == 4 and W_PAIR <= 4:
            arrived(("w", block, 4, "u"), ("w", block, 4, "d"))
        elif far == 4:
            arrived(("w", block, 4, "u" if block == "a" else "d"))
        elif far:
            arrived(("w", block, far, "d" if relative > 0 else "u"))

    def w_pair(relative):
        w_arrived("a", relative)
        place = AT[relative]
        block = wbuf.at[place, row["a"]]
        send(("wz", place), block, block, to_pair)

    def w_core(relative):
        w_arrived("a", relative)
        w_arrived("b", relative)
        place = AT[relative]
        send(("wc", place), wbuf.at[place, 2:4], wbuf.at[place, 0:2], to_core)

    spans = (slice(0, 256), slice(256, 512))
    mine = pl.ds(pl.multiple_of(parity * 64, 64), 64)
    other = pl.ds(pl.multiple_of(64 - parity * 64, 64), 64)

    def kv_start():
        send("kv", kv_send, kv_recv, to_partner)

    def kv_ready():
        arrived("kv")
        loads[4].wait()
        k_turned[mine] = kv_send[0:64]
        v_turned[mine] = kv_send[64:128]
        k_turned[other] = kv_recv[0:64]
        v_turned[other] = kv_recv[64:128]
        k_full[...] = k_turned[...].astype(F32).T.astype(BF16)
        v_full[...] = v_turned[...].astype(F32).T.astype(BF16)

    def forward(head):
        columns = slice(head * 128, head * 128 + 128)
        for span in spans:
            length = span.stop
            scores = nt(k_full[0:length], q_ref[span, columns]) * scale
            key_at = lax.broadcasted_iota(jnp.int32, (length, 256), 0)
            query_at = lax.broadcasted_iota(jnp.int32, (length, 256), 1) + span.start
            scores = jnp.where(key_at <= query_at, scores, -jnp.inf)
            powers = jnp.exp(scores - jnp.max(scores, axis=0, keepdims=True))
            part = powers * (1.0 / jnp.sum(powers, axis=0, keepdims=True))
            probs[head, 0:length, span] = part
            att[columns, span] = nn(v_turned[:, 0:length], part.astype(BF16)).astype(BF16)

    def backward_values():
        for head in range(4):
            columns = slice(head * 128, head * 128 + 128)
            for span in spans[::-1]:
                length = span.stop
                part = nn(probs[head, 0:length, span].astype(BF16), grad_att[span, columns])
                if head == 0 and length == 512:
                    value_acc[...] = part
                else:
                    value_acc[0:length] += part
        value_part[...] = value_acc[...].T.astype(BF16)

    def backward_keys(at):
        span = spans[at]
        length = span.stop
        for head in range(4):
            columns = slice(head * 128, head * 128 + 128)
            part = probs[head, 0:length, span]
            dprobs = nt(v_full[0:length], grad_att[span, columns])
            delta = jnp.sum(part * dprobs, axis=0, keepdims=True)
            dscores = (part * (dprobs - delta) * scale).astype(BF16)
            gq_ref[span, columns] = nn(k_turned[:, 0:length], dscores).T.astype(BF16)
            product = nn(dscores, q_ref[span, columns])
            if head == 0 and at == 1:
                key_acc[...] = product
            else:
                key_acc[0:length] += product
        key_part[:, span] = key_acc[span].T.astype(BF16)
        store(gq_ref.at[span], gq_out.at[span])

    def part_start(which):
        if which == 0:
            send(("part", 0), value_part.at[other], value_recv, to_partner)
        else:
            span = spans[2 - which]
            send(("part", which), key_part.at[other, span], key_recv.at[:, span], to_partner)

    def parts_done():
        arrived(("part", 0), ("part", 1), ("part", 2))
        gk_ref[...] = (key_part[mine].astype(F32) + key_recv[...].astype(F32)).astype(BF16)
        gv_ref[...] = (value_part[mine].astype(F32) + value_recv[...].astype(F32)).astype(BF16)
        store(gk_ref, gk_out)
        store(gv_ref, gv_out)

    summed = []

    def gather_term(place):
        g_done(place)
        arrived(("wc", place))
        for half in range(2):
            columns = slice(half * 256, half * 256 + 256)
            product = nn(
                gbuf[place].reshape(512, 512), wbuf[place, :, :, columns].reshape(512, 256)
            )
            if not summed:
                total[:, columns] = product
            elif len(summed) < 7:
                total[:, columns] += product
            else:
                grad_att[:, columns] = (total[:, columns] + product).astype(BF16)
        summed.append(place)

    def weight_term(place):
        g_done(place)
        features = gbuf[place].reshape(512, 512)
        product = nn(att[...], features[:, 0:256])
        core_send[place, 0] = product[:, 0:128].astype(BF16)
        core_send[place, 1] = product[:, 128:256].astype(BF16)

    def core_start(place):
        send(("core", place), core_send.at[place], core_recv.at[place], to_core)
        features = gbuf[place].reshape(512, 512)
        product = nn(att[...], features[:, 256:512])
        terms[place, 0] = product[:, 0:128]
        terms[place, 1] = product[:, 128:256]

    at_of = {"a": zl, "b": 1 - zl}

    def ring(block, place):
        relative = ORDER[place]
        far = abs(relative)
        at = at_of[block]
        arrived(("core", place))
        partial = terms[place, at] + core_recv[place, at].astype(F32)
        if block == "a" and relative and far >= PAIR:
            arrived(("pair", place))
            partial += z_recv[place].astype(F32)
        if relative:
            y_send[place, at] = partial.astype(BF16)
        for way, sign in (("u", 1), ("d", -1)):
            if relative * sign < 0 or relative == 4:
                continue
            rows, slot = slice(0, 512), ABOVE if relative == 0 and way == "d" else place
            if far == 3 and PAIR <= 4:
                rows = slice(0, 256) if way == "u" else slice(256, 512)
                comes = block == "a"
            elif far == 3:
                comes = block == ("a" if way == "u" else "b")
            else:
                comes = block == "a" or far + 1 < PAIR
            if not comes:
                continue
            arrived(("ring", block, sign * (far + 1), way))
            if far == 3 and PAIR <= 4:
                y_send[place, at, rows] = (partial[rows] + y_recv[slot, at, rows].astype(F32)).astype(BF16)
            else:
                partial += y_recv[slot, at].astype(F32)
                if relative:
                    y_send[place, at] = partial.astype(BF16)
        if block == "b" and (relative == 0 or far >= PAIR):
            z_send[place] = partial.astype(BF16)
        elif relative == 0:
            terms[place, at] = partial

    def ring_start(block, place, way):
        relative = -4 if ORDER[place] == 4 and way == "d" else ORDER[place]
        at = at_of[block]
        rows = slice(0, 512)
        if relative in (4, -4) and PAIR <= 4:
            rows = slice(0, 256) if way == "u" else slice(256, 512)
        if way == "u":
            slot = AT[relative - 1]
        else:
            slot = ABOVE if relative == -1 else AT[relative + 1]
        send(("ring", block, relative, way), y_send.at[place, at, rows], y_recv.at[slot, at, rows], to_y[way])

    def pair_start(place):
        send(("pair", place), z_send.at[place], z_recv.at[place], to_pair)

    def ring_done():
        place = AT[0]
        arrived(("pair", place))
        gw_ref[...] = (terms[place, zl] + z_recv[place].astype(F32)).T.astype(BF16)
        store(gw_ref, gw_out)

    g_x1(0, "d", "own")
    g_x1(0, "u", "own")
    g_x1(1, "d", "own")
    g_x1(1, "u", "own")
    g_z1(0, "d")
    g_z1(0, "u")
    w_pair(0)
    g_z1(1, "d")
    w_hop("a", 1, "d")
    w_hop("a", 1, "u")
    g_x1(2, "d", "own")
    g_x1(2, "u", "own")
    g_x1(3, "d", "own")
    g_x1(3, "u", "own")
    g_z1(2, "d")
    kv_start()
    g_x1(4, "d", "own")
    g_x1(4, "u", "own")
    g_x1(5, "d", "own")
    g_x1(5, "u", "own")
    g_z1(3, "d")
    g_x2(0, "d", "own")
    g_x2(0, "u", "own")
    g_x2(1, "d", "own")
    g_x2(1, "u", "own")
    g_z1(4, "d")
    g_z1(1, "u")
    g_x2(2, "d", "own")
    g_x2(2, "u", "own")
    g_x2(3, "d", "own")
    w_hop("a", 2, "d")
    w_hop("a", 2, "u")
    g_x1(0, "d", "up")
    g_x1(0, "u", "down")
    g_x1(0, "u", "up")
    g_x1(0, "d", "down")
    g_z2(0, "d")
    g_x2(3, "u", "own")
    g_x2(4, "d", "own")
    g_x2(4, "u", "own")
    g_x1(1, "d", "up")
    w_hop("b", 1, "d")
    w_hop("b", 1, "u")
    w_core(0)
    g_x1(1, "u", "up")
    g_x2(5, "d", "own")
    g_z2(1, "d")
    g_z2(0, "u")
    g_x2(5, "u", "own")
    g_z1(5, "d")
    g_x1(2, "d", "up")
    g_x1(2, "u", "up")
    g_z2(2, "d")
    g_x2(0, "u", "down")
    g_z1(2, "u")
    g_x2(0, "d", "up")
    g_x2(0, "u", "up")
    g_z1(3, "u")
    g_x2(0, "d", "down")
    g_x1(3, "d", "up")
    g_x1(3, "u", "up")
    g_z2(3, "d")
    w_hop("a", 3, "d")
    w_hop("a", 3, "u")
    g_x2(1, "d", "up")
    g_x2(1, "u", "up")
    g_z1(6, "d")
    g_z1(4, "u")
    g_x1(4, "d", "up")
    g_x1(4, "u", "up")
    kv_ready()
    forward(0)
    g_z2(4, "d")
    g_x2(2, "d", "up")
    g_x2(2, "u", "up")
    forward(1)
    g_z1(5, "u")
    g_x1(1, "d", "down")
    g_x1(1, "u", "down")
    forward(2)
    w_hop("b", 2, "d")
    w_hop("b", 2, "u")
    g_x2(3, "u", "up")
    w_core(1)
    w_core(-1)
    g_x1(0, "d", "far")
    g_x1(0, "u", "far")
    g_x2(3, "d", "up")
    g_z1(7, "d")
    forward(3)
    g_z2(1, "u")
    g_z2(5, "d")
    g_x1(5, "d", "up")
    g_x1(5, "u", "up")
    g_x2(4, "d", "up")
    g_x2(4, "u", "up")
    g_x1(2, "u", "down")
    g_x1(2, "d", "down")
    g_z2(2, "u")
    w_hop("a", 4, "u")
    g_z1(6, "u")
    g_x2(1, "d", "down")
    g_x2(1, "u", "down")
    g_x1(3, "d", "down")
    g_x1(3, "u", "down")
    g_z2(3, "u")
    g_x2(0, "d", "far")
    g_z2(6, "d")
    g_x2(0, "u", "far")
    g_x1(4, "d", "down")
    g_x1(4, "u", "down")
    g_x2(5, "d", "up")
    g_x2(5, "u", "up")
    g_z2(4, "u")
    w_hop("b", 3, "d")
    w_hop("b", 3, "u")
    w_core(2)
    w_core(-2)
    g_x2(2, "u", "down")
    g_x2(2, "d", "down")
    g_z1(7, "u")
    g_z2(7, "d")
    g_x1(5, "d", "down")
    g_x1(5, "u", "down")
    g_z2(5, "u")
    g_x2(3, "d", "down")
    g_x1(1, "d", "far")
    g_x1(1, "u", "far")
    g_x2(3, "u", "down")
    weight_term(0)
    core_start(0)
    g_x1(2, "d", "far")
    g_x1(2, "u", "far")
    g_x2(4, "d", "down")
    g_x2(4, "u", "down")
    g_z2(6, "u")
    ring("b", 0)
    pair_start(0)
    g_x2(5, "d", "down")
    g_x2(5, "u", "down")
    g_x1(3, "d", "far")
    g_x1(3, "u", "far")
    w_hop("b", 4, "d")
    g_x2(1, "u", "far")
    w_core(3)
    w_core(-3)
    g_x1(4, "d", "far")
    g_x2(1, "d", "far")
    g_x1(4, "u", "far")
    g_x2(2, "d", "far")
    g_x2(2, "u", "far")
    g_z2(7, "u")
    g_x1(5, "d", "far")
    g_x1(5, "u", "far")
    g_x2(3, "d", "far")
    g_x2(3, "u", "far")
    g_x1(6, "d")
    g_x1(6, "u")
    g_x2(4, "d", "far")
    weight_term(1)
    core_start(1)
    g_x2(4, "u", "far")
    weight_term(2)
    core_start(2)
    gather_term(1)
    ring("a", 0)
    ring_start("a", 0, "d")
    ring_start("a", 0, "u")
    w_core(4)
    gather_term(2)
    g_x2(5, "d", "far")
    g_x2(5, "u", "far")
    ring("b", 1)
    ring_start("b", 1, "u")
    weight_term(3)
    core_start(3)
    gather_term(3)
    ring("b", 2)
    ring_start("b", 2, "d")
    g_x1(7, "d")
    g_x1(7, "u")
    gather_term(0)
    g_x2(6, "d")
    g_x2(6, "u")
    ring("a", 2)
    ring_start("a", 2, "d")
    ring("a", 1)
    ring_start("a", 1, "u")
    weight_term(4)
    core_start(4)
    weight_term(5)
    core_start(5)
    gather_term(4)
    gather_term(5)
    ring("b", 3)
    ring_start("b", 3, "u")
    ring("b", 4)
    ring_start("b", 4, "d")
    g_x2(7, "d")
    g_x2(7, "u")
    weight_term(6)
    core_start(6)
    gather_term(6)
    ring("a", 3)
    ring_start("a", 3, "u")
    ring("a", 4)
    ring_start("a", 4, "d")
    gather_term(7)
    weight_term(7)
    core_start(7)
    ring("b", 5)
    ring_start("b", 5, "u")
    ring("b", 6)
    ring_start("b", 6, "d")
    backward_values()
    part_start(0)
    backward_keys(1)
    part_start(1)
    backward_keys(0)
    part_start(2)
    ring("a", 5)
    ring_start("a", 5, "u")
    ring("a", 6)
    ring_start("a", 6, "d")
    ring("b", 7)
    pair_start(7)
    parts_done()
    ring("a", 7)
    ring_done()
    for copy in copies.values():
        copy.wait_send()
    for copy in stores:
        copy.wait()


def place_results(*refs):
    for i in range(4):
        refs[i + 4][...] = refs[i][...]


def body(queries, keys, values, grad_out, out_weight):
    vmem = pl.BlockSpec(memory_space=pltpu.VMEM)
    anywhere = pl.BlockSpec(memory_space=pl.ANY)
    grad_q, grad_k, grad_v, grad_weight = pl.pallas_call(
        kernel,
        out_shape=(
            jax.ShapeDtypeStruct((512, 512), BF16),
            jax.ShapeDtypeStruct((64, 512), BF16),
            jax.ShapeDtypeStruct((64, 512), BF16),
            jax.ShapeDtypeStruct((128, 512), BF16),
        ),
        in_specs=[anywhere] * 5,
        out_specs=(anywhere,) * 4,
        scratch_shapes=[
            pltpu.VMEM((512, 512), BF16),
            pltpu.VMEM((32, 4096), BF16),
            pltpu.VMEM((512, 512), BF16),
            pltpu.VMEM((64, 512), BF16),
            pltpu.VMEM((64, 512), BF16),
            pltpu.VMEM((128, 512), BF16),
            pltpu.SemaphoreType.DMA((10,)),
            pltpu.VMEM((8, 4, 128, 512), BF16),
            pltpu.VMEM((8, 4, 128, 512), BF16),
            pltpu.VMEM((128, 512), BF16),
            pltpu.VMEM((128, 512), BF16),
            pltpu.VMEM((512, 128), BF16),
            pltpu.VMEM((512, 128), BF16),
            pltpu.VMEM((128, 512), BF16),
            pltpu.VMEM((128, 512), BF16),
            pltpu.VMEM((4, 512, 512), F32),
            pltpu.VMEM((512, 512), BF16),
            pltpu.VMEM((512, 512), F32),
            pltpu.VMEM((512, 512), BF16),
            pltpu.VMEM((8, 2, 512, 128), F32),
            pltpu.VMEM((8, 2, 512, 128), BF16),
            pltpu.VMEM((8, 2, 512, 128), BF16),
            pltpu.VMEM((8, 2, 512, 128), BF16),
            pltpu.VMEM((9, 2, 512, 128), BF16),
            pltpu.VMEM((8, 512, 128), BF16),
            pltpu.VMEM((8, 512, 128), BF16),
            pltpu.VMEM((512, 128), F32),
            pltpu.VMEM((512, 128), F32),
            pltpu.VMEM((128, 512), BF16),
            pltpu.VMEM((128, 512), BF16),
            pltpu.VMEM((64, 512), BF16),
            pltpu.VMEM((64, 512), BF16),
            pltpu.SemaphoreType.DMA((N_COPIES,)),
            pltpu.SemaphoreType.DMA((N_COPIES,)),
        ],
        compiler_params=pltpu.CompilerParams(
            collective_id=0, has_side_effects=True, vmem_limit_bytes=56 * 1024 * 1024
        ),
        cost_estimate=pl.CostEstimate(
            flops=6_000_000_000, bytes_accessed=4_000_000, transcendentals=1_000_000
        ),
    )(queries, keys.T, values.T, grad_out, out_weight)
    results = (grad_q, grad_k, grad_v, grad_weight)
    grad_q, grad_k, grad_v, grad_weight = pl.pallas_call(
        place_results,
        out_shape=tuple(jax.ShapeDtypeStruct(array.shape, array.dtype) for array in results),
        in_specs=[vmem] * 4,
        out_specs=(vmem,) * 4,
        cost_estimate=pl.CostEstimate(flops=0, bytes_accessed=1_600_000, transcendentals=0),
    )(*results)
    return grad_q, grad_k.T, grad_v.T, grad_weight


def solution(mesh):
    placed = (
        P("dp", "tensor"),
        P("dp", "tensor"),
        P("dp", "tensor"),
        P(("dp", "tensor"), None),
        P("dp", "tensor"),
    )
    return jax.shard_map(
        body,
        mesh=mesh,
        in_specs=placed,
        out_specs=(P("dp", "tensor"), P("dp", "tensor"), P("dp", "tensor"), P("dp", "tensor")),
        check_vma=False,
    )
```

```python
import jax
import jax.numpy as jnp
from jax import lax
from jax.experimental import pallas as pl
from jax.experimental.pallas import tpu as pltpu
from jax.sharding import PartitionSpec as P

HEAD_DIM = 128
MESH = pl.DeviceIdType.MESH
F32 = jnp.float32
BF16 = jnp.bfloat16

ORDER = (4, 3, -3, 2, -2, 1, -1, 0)
AT = {relative: place for place, relative in enumerate(ORDER)}
AT[-4] = AT[4]
ABOVE = 8

NX, NZ, NY = 4, 4, 8
N_COPIES = 224

PAIR, W_PAIR = 4, 5

WAY = tuple('PPPPPPZZ')


def nt(a, b):
    return lax.dot_general(a, b, (((1,), (1,)), ((), ())), preferred_element_type=F32)


def nn(a, b):
    return lax.dot_general(a, b, (((1,), (0,)), ((), ())), preferred_element_type=F32)


def kernel(
    q_in, k_in, v_in, g_in, w_in,
    gq_out, gk_out, gv_out, gw_out,
    q_ref, g_ref, gq_ref, gk_ref, gv_ref, gw_ref, local_sem,
    gbuf, wbuf, kv_send, kv_recv, k_full, v_full, k_turned, v_turned,
    probs, att, total, grad_att, terms, core_send, core_recv, y_send, y_recv,
    z_send, z_recv, key_acc, value_acc, key_part, value_part, key_recv, value_recv, send_sem, recv_sem,
):
    scale = HEAD_DIM ** (-0.5)
    dp = lax.axis_index("dp")
    tensor = lax.axis_index("tensor")
    core = lax.rem(dp, 2)
    y = lax.rem(dp // 2, NY)
    zl = dp // (2 * NY)
    x = tensor // NZ
    zh = lax.rem(tensor, NZ)
    parity = lax.rem(tensor, 2)

    def device(core=core, y=y, zl=zl, x=x, zh=zh):
        return ((zl * NY + y) * 2 + core, x * NZ + zh)

    x_up, x_down = lax.rem(x + 1, NX), lax.rem(x + NX - 1, NX)
    z_up, z_down = lax.rem(zh + 1, NZ), lax.rem(zh + NZ - 1, NZ)
    to_x_up, to_x_down = device(x=x_up), device(x=x_down)
    to_z_up, to_z_down = device(zh=z_up), device(zh=z_down)
    to_y_up = device(y=lax.rem(y + 1, NY))
    to_y_down = device(y=lax.rem(y + NY - 1, NY))
    to_pair = device(zl=1 - zl)
    to_core = device(core=1 - core)
    to_partner = (dp, tensor + 1 - 2 * parity)

    barrier = pltpu.get_barrier_semaphore()
    for target in (to_x_up, to_x_down, to_z_up, to_z_down, to_y_up, to_y_down, to_pair, to_core):
        pl.semaphore_signal(barrier, inc=1, device_id=target, device_id_type=MESH)

    copies = {}

    def send(name, source, target, to):
        index = len(copies)
        copy = pltpu.make_async_remote_copy(
            src_ref=source, dst_ref=target, send_sem=send_sem.at[index], recv_sem=recv_sem.at[index],
            device_id=to, device_id_type=MESH,
        )
        copy.start()
        copies[name] = copy

    waited = set()

    def arrived(*names):
        for name in names:
            if name not in waited:
                copies[name].wait_recv()
                waited.add(name)

    loads = [
        pltpu.make_async_copy(source, target, local_sem.at[i])
        for i, (source, target) in enumerate((
            (g_in, g_ref), (k_in, kv_send.at[0:64]), (v_in, kv_send.at[64:128]),
            (w_in, wbuf.at[AT[0], 2 + zl]), (q_in, q_ref),
        ))
    ]
    for load in loads:
        load.start()
    stores = []

    def store(source, target):
        copy = pltpu.make_async_copy(source, target, local_sem.at[len(loads) + len(stores)])
        copy.start()
        stores.append(copy)

    loads[0].wait()
    own_rows = pl.ds(pl.multiple_of(zh * 32, 32), 32)
    for place, relative in enumerate(ORDER):
        column = lax.rem(y + relative + NY, NY)
        for slot in range(4):
            of_core = core if slot >= 2 else 1 - core
            block = ((slot % 2) * NY + column) * 2 + of_core
            gbuf[place, x, own_rows, slot * 128 : (slot + 1) * 128] = g_ref[
                :, pl.ds(pl.multiple_of(block * 128, 128), 128)
            ]
    for load in loads[1:4]:
        load.wait()
    pl.semaphore_wait(barrier, 8)

    def z_rows(at, first, count):
        return pl.ds(pl.multiple_of(at * 32 + first, 16), count)

    to_x, to_y, to_z = (
        {"u": to_x_up, "d": to_x_down}, {"u": to_y_up, "d": to_y_down}, {"u": to_z_up, "d": to_z_down},
    )
    from_x, from_z = {"u": x_down, "d": x_up}, {"u": z_down, "d": z_up}
    kept = {"u": 0, "d": 16}
    pieces = {"own": zh, "down": z_down, "up": z_up, "far": lax.rem(zh + 2, NZ)}
    before = {"own": (), "down": ("u",), "up": ("d",), "far": ("u", "d")}

    def g_z1(place, way):
        if WAY[place] == "X":
            arrived(("x2", place, "u", None), ("x2", place, "d", None))
            block = gbuf.at[place, :, z_rows(zh, 0, 32)]
        else:
            block = gbuf.at[place, x, z_rows(zh, 0, 32)]
        send(("z1", place, way), block, block, to_z[way])

    def g_z2(place, way):
        arrived(("z1", place, way))
        rows = z_rows(from_z[way], kept[way], 16)
        block = gbuf.at[place, :, rows] if WAY[place] == "X" else gbuf.at[place, x, rows]
        send(("z2", place, way), block, block, to_z[way])

    def g_x1(place, way, piece=None):
        if WAY[place] == "X":
            block = gbuf.at[place, x, z_rows(zh, 0, 32)]
        elif piece is None:
            arrived(("z2", place, "u"), ("z2", place, "d"))
            block = gbuf.at[place, x]
        else:
            kind = "z2" if piece == "far" else "z1"
            arrived(*((kind, place, which) for which in before[piece]))
            block = gbuf.at[place, x, z_rows(pieces[piece], 0, 32)]
        send(("x1", place, way, piece), block, block, to_x[way])

    def g_x2(place, way, piece=None):
        arrived(("x1", place, way, piece))
        if WAY[place] == "X":
            rows = z_rows(zh, kept[way], 16)
        elif piece is None:
            rows = pl.ds(kept[way] * 4, 64)
        else:
            rows = z_rows(pieces[piece], kept[way], 16)
        block = gbuf.at[place, from_x[way], rows]
        send(("x2", place, way, piece), block, block, to_x[way])

    def g_done(place):
        for way in ("u", "d"):
            if WAY[place] == "X":
                arrived(("z2", place, way))
            elif WAY[place] == "P":
                arrived(*(("x2", place, way, piece) for piece in pieces))
            else:
                arrived(("x2", place, way, None))

    row = {"a": 2 + zl, "b": 3 - zl}

    def w_hop(block, step, way):
        if step > 1:
            arrived(("w", block, step - 1, way))
        elif block == "b":
            arrived(("wz", AT[0]))
        relative = (1 - step) if way == "u" else (step - 1)
        source = wbuf.at[AT[relative], row[block]]
        target = wbuf.at[AT[relative - 1 if way == "u" else relative + 1], row[block]]
        if step == 4 and W_PAIR <= 4:
            rows = slice(0, 64) if way == "u" else slice(64, 128)
            source, target = source.at[rows], target.at[rows]
        send(("w", block, step, way), source, target, to_y[way])

    def w_arrived(block, relative):
        far = abs(relative)
        if block == "b" and (relative == 0 or far >= W_PAIR):
            arrived(("wz", AT[relative]))
        elif far == 4 and W_PAIR <= 4:
            arrived(("w", block, 4, "u"), ("w", block, 4, "d"))
        elif far == 4:
            arrived(("w", block, 4, "u" if block == "a" else "d"))
        elif far:
            arrived(("w", block, far, "d" if relative > 0 else "u"))

    def w_pair(relative):
        w_arrived("a", relative)
        place = AT[relative]
        block = wbuf.at[place, row["a"]]
        send(("wz", place), block, block, to_pair)

    def w_core(relative):
        w_arrived("a", relative)
        w_arrived("b", relative)
        place = AT[relative]
        send(("wc", place), wbuf.at[place, 2:4], wbuf.at[place, 0:2], to_core)

    spans = (slice(0, 256), slice(256, 512))
    mine = pl.ds(pl.multiple_of(parity * 64, 64), 64)
    other = pl.ds(pl.multiple_of(64 - parity * 64, 64), 64)

    def kv_start():
        send("kv", kv_send, kv_recv, to_partner)

    def kv_ready():
        arrived("kv")
        loads[4].wait()
        k_turned[mine] = kv_send[0:64]
        v_turned[mine] = kv_send[64:128]
        k_turned[other] = kv_recv[0:64]
        v_turned[other] = kv_recv[64:128]
        k_full[...] = k_turned[...].astype(F32).T.astype(BF16)
        v_full[...] = v_turned[...].astype(F32).T.astype(BF16)

    def forward(head):
        columns = slice(head * 128, head * 128 + 128)
        for span in spans:
            length = span.stop
            scores = nt(k_full[0:length], q_ref[span, columns]) * scale
            key_at = lax.broadcasted_iota(jnp.int32, (length, 256), 0)
            query_at = lax.broadcasted_iota(jnp.int32, (length, 256), 1) + span.start
            scores = jnp.where(key_at <= query_at, scores, -jnp.inf)
            powers = jnp.exp(scores - jnp.max(scores, axis=0, keepdims=True))
            part = powers * (1.0 / jnp.sum(powers, axis=0, keepdims=True))
            probs[head, 0:length, span] = part
            att[columns, span] = nn(v_turned[:, 0:length], part.astype(BF16)).astype(BF16)

    def backward_values():
        for head in range(4):
            columns = slice(head * 128, head * 128 + 128)
            for span in spans[::-1]:
                length = span.stop
                part = nn(probs[head, 0:length, span].astype(BF16), grad_att[span, columns])
                if head == 0 and length == 512:
                    value_acc[...] = part
                else:
                    value_acc[0:length] += part
        value_part[...] = value_acc[...].T.astype(BF16)

    def backward_keys(at):
        span = spans[at]
        length = span.stop
        for head in range(4):
            columns = slice(head * 128, head * 128 + 128)
            part = probs[head, 0:length, span]
            dprobs = nt(v_full[0:length], grad_att[span, columns])
            delta = jnp.sum(part * dprobs, axis=0, keepdims=True)
            dscores = (part * (dprobs - delta) * scale).astype(BF16)
            gq_ref[span, columns] = nn(k_turned[:, 0:length], dscores).T.astype(BF16)
            product = nn(dscores, q_ref[span, columns])
            if head == 0 and at == 1:
                key_acc[...] = product
            else:
                key_acc[0:length] += product
        key_part[:, span] = key_acc[span].T.astype(BF16)
        store(gq_ref.at[span], gq_out.at[span])

    def part_start(which):
        if which == 0:
            send(("part", 0), value_part.at[other], value_recv, to_partner)
        else:
            span = spans[2 - which]
            send(("part", which), key_part.at[other, span], key_recv.at[:, span], to_partner)

    def parts_done():
        arrived(("part", 0), ("part", 1), ("part", 2))
        gk_ref[...] = (key_part[mine].astype(F32) + key_recv[...].astype(F32)).astype(BF16)
        gv_ref[...] = (value_part[mine].astype(F32) + value_recv[...].astype(F32)).astype(BF16)
        store(gk_ref, gk_out)
        store(gv_ref, gv_out)

    summed = []

    def gather_term(place):
        g_done(place)
        arrived(("wc", place))
        for half in range(2):
            columns = slice(half * 256, half * 256 + 256)
            product = nn(
                gbuf[place].reshape(512, 512), wbuf[place, :, :, columns].reshape(512, 256)
            )
            if not summed:
                total[:, columns] = product
            elif len(summed) < 7:
                total[:, columns] += product
            else:
                grad_att[:, columns] = (total[:, columns] + product).astype(BF16)
        summed.append(place)

    def weight_term(place):
        g_done(place)
        features = gbuf[place].reshape(512, 512)
        product = nn(att[...], features[:, 0:256])
        core_send[place, 0] = product[:, 0:128].astype(BF16)
        core_send[place, 1] = product[:, 128:256].astype(BF16)

    def core_start(place):
        send(("core", place), core_send.at[place], core_recv.at[place], to_core)
        features = gbuf[place].reshape(512, 512)
        product = nn(att[...], features[:, 256:512])
        terms[place, 0] = product[:, 0:128]
        terms[place, 1] = product[:, 128:256]

    at_of = {"a": zl, "b": 1 - zl}

    def ring(block, place):
        relative = ORDER[place]
        far = abs(relative)
        at = at_of[block]
        arrived(("core", place))
        partial = terms[place, at] + core_recv[place, at].astype(F32)
        if block == "a" and relative and far >= PAIR:
            arrived(("pair", place))
            partial += z_recv[place].astype(F32)
        if relative:
            y_send[place, at] = partial.astype(BF16)
        for way, sign in (("u", 1), ("d", -1)):
            if relative * sign < 0 or relative == 4:
                continue
            rows, slot = slice(0, 512), ABOVE if relative == 0 and way == "d" else place
            if far == 3 and PAIR <= 4:
                rows = slice(0, 256) if way == "u" else slice(256, 512)
                comes = block == "a"
            elif far == 3:
                comes = block == ("a" if way == "u" else "b")
            else:
                comes = block == "a" or far + 1 < PAIR
            if not comes:
                continue
            arrived(("ring", block, sign * (far + 1), way))
            if far == 3 and PAIR <= 4:
                y_send[place, at, rows] = (partial[rows] + y_recv[slot, at, rows].astype(F32)).astype(BF16)
            else:
                partial += y_recv[slot, at].astype(F32)
                if relative:
                    y_send[place, at] = partial.astype(BF16)
        if block == "b" and (relative == 0 or far >= PAIR):
            z_send[place] = partial.astype(BF16)
        elif relative == 0:
            terms[place, at] = partial

    def ring_start(block, place, way):
        relative = -4 if ORDER[place] == 4 and way == "d" else ORDER[place]
        at = at_of[block]
        rows = slice(0, 512)
        if relative in (4, -4) and PAIR <= 4:
            rows = slice(0, 256) if way == "u" else slice(256, 512)
        if way == "u":
            slot = AT[relative - 1]
        else:
            slot = ABOVE if relative == -1 else AT[relative + 1]
        send(("ring", block, relative, way), y_send.at[place, at, rows], y_recv.at[slot, at, rows], to_y[way])

    def pair_start(place):
        send(("pair", place), z_send.at[place], z_recv.at[place], to_pair)

    def ring_done():
        place = AT[0]
        arrived(("pair", place))
        gw_ref[...] = (terms[place, zl] + z_recv[place].astype(F32)).T.astype(BF16)
        store(gw_ref, gw_out)

    g_x1(0, "d", "own")
    g_x1(0, "u", "own")
    g_x1(1, "d", "own")
    g_x1(1, "u", "own")
    g_z1(0, "d")
    g_z1(0, "u")
    w_pair(0)
    g_z1(1, "d")
    w_hop("a", 1, "d")
    w_hop("a", 1, "u")
    g_x1(2, "d", "own")
    g_x1(2, "u", "own")
    g_x1(3, "d", "own")
    g_x1(3, "u", "own")
    g_z1(2, "d")
    kv_start()
    g_x1(4, "d", "own")
    g_x1(4, "u", "own")
    g_x1(5, "d", "own")
    g_x1(5, "u", "own")
    g_z1(3, "d")
    g_x2(0, "d", "own")
    g_x2(0, "u", "own")
    g_x2(1, "d", "own")
    g_x2(1, "u", "own")
    g_z1(4, "d")
    g_z1(1, "u")
    g_x2(2, "d", "own")
    g_x2(2, "u", "own")
    g_x2(3, "d", "own")
    w_hop("a", 2, "d")
    w_hop("a", 2, "u")
    g_x1(0, "d", "up")
    g_x1(0, "u", "down")
    g_x1(0, "u", "up")
    g_x1(0, "d", "down")
    g_z2(0, "d")
    g_x2(3, "u", "own")
    g_x2(4, "d", "own")
    g_x2(4, "u", "own")
    g_x1(1, "d", "up")
    w_hop("b", 1, "d")
    w_hop("b", 1, "u")
    w_core(0)
    g_x1(1, "u", "up")
    g_x2(5, "d", "own")
    g_z2(1, "d")
    g_z2(0, "u")
    g_x2(5, "u", "own")
    g_z1(5, "d")
    g_x1(2, "d", "up")
    g_x1(2, "u", "up")
    g_z2(2, "d")
    g_x2(0, "u", "down")
    g_z1(2, "u")
    g_x2(0, "d", "up")
    g_x2(0, "u", "up")
    g_z1(3, "u")
    g_x2(0, "d", "down")
    g_x1(3, "d", "up")
    g_x1(3, "u", "up")
    g_z2(3, "d")
    w_hop("a", 3, "d")
    w_hop("a", 3, "u")
    g_x2(1, "d", "up")
    g_x2(1, "u", "up")
    g_z1(6, "d")
    g_z1(4, "u")
    g_x1(4, "d", "up")
    g_x1(4, "u", "up")
    kv_ready()
    forward(0)
    g_z2(4, "d")
    g_x2(2, "d", "up")
    g_x2(2, "u", "up")
    forward(1)
    g_z1(5, "u")
    g_x1(1, "d", "down")
    g_x1(1, "u", "down")
    forward(2)
    w_hop("b", 2, "d")
    w_hop("b", 2, "u")
    g_x2(3, "u", "up")
    w_core(1)
    w_core(-1)
    g_x1(0, "d", "far")
    g_x1(0, "u", "far")
    g_x2(3, "d", "up")
    g_z1(7, "d")
    forward(3)
    g_z2(1, "u")
    g_z2(5, "d")
    g_x1(5, "d", "up")
    g_x1(5, "u", "up")
    g_x2(4, "d", "up")
    g_x2(4, "u", "up")
    g_x1(2, "u", "down")
    g_x1(2, "d", "down")
    g_z2(2, "u")
    w_hop("a", 4, "u")
    g_z1(6, "u")
    g_x2(1, "d", "down")
    g_x2(1, "u", "down")
    g_x1(3, "d", "down")
    g_x1(3, "u", "down")
    g_z2(3, "u")
    g_x2(0, "d", "far")
    g_z2(6, "d")
    g_x2(0, "u", "far")
    g_x1(4, "d", "down")
    g_x1(4, "u", "down")
    g_x2(5, "d", "up")
    g_x2(5, "u", "up")
    g_z2(4, "u")
    w_hop("b", 3, "d")
    w_hop("b", 3, "u")
    w_core(2)
    w_core(-2)
    g_x2(2, "u", "down")
    g_x2(2, "d", "down")
    g_z1(7, "u")
    g_z2(7, "d")
    g_x1(5, "d", "down")
    g_x1(5, "u", "down")
    g_z2(5, "u")
    g_x2(3, "d", "down")
    g_x1(1, "d", "far")
    g_x1(1, "u", "far")
    g_x2(3, "u", "down")
    weight_term(0)
    core_start(0)
    g_x1(2, "d", "far")
    g_x1(2, "u", "far")
    g_x2(4, "d", "down")
    g_x2(4, "u", "down")
    g_z2(6, "u")
    ring("b", 0)
    pair_start(0)
    g_x2(5, "d", "down")
    g_x2(5, "u", "down")
    g_x1(3, "d", "far")
    g_x1(3, "u", "far")
    w_hop("b", 4, "d")
    g_x2(1, "u", "far")
    w_core(3)
    w_core(-3)
    g_x1(4, "d", "far")
    g_x2(1, "d", "far")
    g_x1(4, "u", "far")
    g_x2(2, "d", "far")
    g_x2(2, "u", "far")
    g_z2(7, "u")
    g_x1(5, "d", "far")
    g_x1(5, "u", "far")
    g_x2(3, "d", "far")
    g_x2(3, "u", "far")
    g_x1(6, "d")
    g_x1(6, "u")
    g_x2(4, "d", "far")
    weight_term(1)
    core_start(1)
    g_x2(4, "u", "far")
    weight_term(2)
    core_start(2)
    gather_term(1)
    ring("a", 0)
    ring_start("a", 0, "d")
    ring_start("a", 0, "u")
    w_core(4)
    gather_term(2)
    g_x2(5, "d", "far")
    g_x2(5, "u", "far")
    ring("b", 1)
    ring_start("b", 1, "u")
    weight_term(3)
    core_start(3)
    gather_term(3)
    ring("b", 2)
    ring_start("b", 2, "d")
    g_x1(7, "d")
    g_x1(7, "u")
    gather_term(0)
    g_x2(6, "d")
    g_x2(6, "u")
    ring("a", 2)
    ring_start("a", 2, "d")
    ring("a", 1)
    ring_start("a", 1, "u")
    weight_term(4)
    core_start(4)
    weight_term(5)
    core_start(5)
    gather_term(4)
    gather_term(5)
    ring("b", 3)
    ring_start("b", 3, "u")
    ring("b", 4)
    ring_start("b", 4, "d")
    g_x2(7, "d")
    g_x2(7, "u")
    weight_term(6)
    core_start(6)
    gather_term(6)
    ring("a", 3)
    ring_start("a", 3, "u")
    ring("a", 4)
    ring_start("a", 4, "d")
    gather_term(7)
    weight_term(7)
    core_start(7)
    ring("b", 5)
    ring_start("b", 5, "u")
    ring("b", 6)
    ring_start("b", 6, "d")
    backward_values()
    part_start(0)
    backward_keys(1)
    part_start(1)
    backward_keys(0)
    part_start(2)
    ring("a", 5)
    ring_start("a", 5, "u")
    ring("a", 6)
    ring_start("a", 6, "d")
    ring("b", 7)
    pair_start(7)
    parts_done()
    ring("a", 7)
    ring_done()
    for copy in copies.values():
        copy.wait_send()
    for copy in stores:
        copy.wait()


def place_results(*refs):
    arrays, results, held, sems = refs[0:4], refs[4:8], refs[8:12], refs[12]
    pieces = [(0, slice(part * 256, part * 256 + 256)) for part in range(2)]
    pieces += [(1, slice(0, 64)), (2, slice(0, 64)), (3, slice(0, 128))]
    inward = [
        pltpu.make_async_copy(arrays[i].at[rows], held[i].at[rows], sems.at[0, at])
        for at, (i, rows) in enumerate(pieces)
    ]
    outward = [
        pltpu.make_async_copy(held[i].at[rows], results[i].at[rows], sems.at[1, at])
        for at, (i, rows) in enumerate(pieces)
    ]
    for copy in inward:
        copy.start()
    for arrival, copy in zip(inward, outward):
        arrival.wait()
        copy.start()
    for copy in outward:
        copy.wait()


def body(queries, keys, values, grad_out, out_weight):
    anywhere = pl.BlockSpec(memory_space=pl.ANY)
    grad_q, grad_k, grad_v, grad_weight = pl.pallas_call(
        kernel,
        out_shape=(
            jax.ShapeDtypeStruct((512, 512), BF16),
            jax.ShapeDtypeStruct((64, 512), BF16),
            jax.ShapeDtypeStruct((64, 512), BF16),
            jax.ShapeDtypeStruct((128, 512), BF16),
        ),
        in_specs=[anywhere] * 5,
        out_specs=(anywhere,) * 4,
        scratch_shapes=[
            pltpu.VMEM((512, 512), BF16),
            pltpu.VMEM((32, 4096), BF16),
            pltpu.VMEM((512, 512), BF16),
            pltpu.VMEM((64, 512), BF16),
            pltpu.VMEM((64, 512), BF16),
            pltpu.VMEM((128, 512), BF16),
            pltpu.SemaphoreType.DMA((10,)),
            pltpu.VMEM((8, 4, 128, 512), BF16),
            pltpu.VMEM((8, 4, 128, 512), BF16),
            pltpu.VMEM((128, 512), BF16),
            pltpu.VMEM((128, 512), BF16),
            pltpu.VMEM((512, 128), BF16),
            pltpu.VMEM((512, 128), BF16),
            pltpu.VMEM((128, 512), BF16),
            pltpu.VMEM((128, 512), BF16),
            pltpu.VMEM((4, 512, 512), F32),
            pltpu.VMEM((512, 512), BF16),
            pltpu.VMEM((512, 512), F32),
            pltpu.VMEM((512, 512), BF16),
            pltpu.VMEM((8, 2, 512, 128), F32),
            pltpu.VMEM((8, 2, 512, 128), BF16),
            pltpu.VMEM((8, 2, 512, 128), BF16),
            pltpu.VMEM((8, 2, 512, 128), BF16),
            pltpu.VMEM((9, 2, 512, 128), BF16),
            pltpu.VMEM((8, 512, 128), BF16),
            pltpu.VMEM((8, 512, 128), BF16),
            pltpu.VMEM((512, 128), F32),
            pltpu.VMEM((512, 128), F32),
            pltpu.VMEM((128, 512), BF16),
            pltpu.VMEM((128, 512), BF16),
            pltpu.VMEM((64, 512), BF16),
            pltpu.VMEM((64, 512), BF16),
            pltpu.SemaphoreType.DMA((N_COPIES,)),
            pltpu.SemaphoreType.DMA((N_COPIES,)),
        ],
        compiler_params=pltpu.CompilerParams(
            collective_id=0, has_side_effects=True, vmem_limit_bytes=56 * 1024 * 1024
        ),
        cost_estimate=pl.CostEstimate(
            flops=6_000_000_000, bytes_accessed=4_000_000, transcendentals=1_000_000
        ),
    )(queries, keys.T, values.T, grad_out, out_weight)
    results = (grad_q, grad_k, grad_v, grad_weight)
    grad_q, grad_k, grad_v, grad_weight = pl.pallas_call(
        place_results,
        out_shape=tuple(jax.ShapeDtypeStruct(array.shape, array.dtype) for array in results),
        in_specs=[anywhere] * 4,
        out_specs=(anywhere,) * 4,
        scratch_shapes=[
            *(pltpu.VMEM(array.shape, array.dtype) for array in results),
            pltpu.SemaphoreType.DMA((2, 5)),
        ],
        cost_estimate=pl.CostEstimate(flops=0, bytes_accessed=1_600_000, transcendentals=0),
    )(*results)
    return grad_q, grad_k.T, grad_v.T, grad_weight


def solution(mesh):
    placed = (
        P("dp", "tensor"),
        P("dp", "tensor"),
        P("dp", "tensor"),
        P(("dp", "tensor"), None),
        P("dp", "tensor"),
    )
    return jax.shard_map(
        body,
        mesh=mesh,
        in_specs=placed,
        out_specs=(P("dp", "tensor"), P("dp", "tensor"), P("dp", "tensor"), P("dp", "tensor")),
        check_vma=False,
    )
```
